128 devices in a mesh: feed: 8 (over y, core), freq: 16 (over x, z).
Axes of the slice: x: 4, y: 4, z: 4, core: 2. Of those that a mesh axis runs over, the one named last changes fastest.
Arguments:
- volts: bfloat16 [2048, 393216], P('feed', 'freq'), may hold values from -6 to 6
- beam_weights: bfloat16 [2, 1024, 2048], P(None, None, 'feed'), may hold values from -0.125 to 0.125
- allocation: int32 [16, 3], replicated, may hold values from -1 to 31, as said below
- beam_order: int32 [1024], replicated, may hold values from 0 to 1023, each once
Outputs:
- visibility: float32 [48, 2, 2048, 2048], P('freq', None, 'feed')
- beam_power: float32 [1024, 48], P('feed', 'freq')
The draws below stay inside these ranges and needn't reach their ends.
Inputs may be any that keep to these rules, and one draw needn't show every extreme that they name: `allocation`: row j lists owner j's channels in slots 0 up to its count and -1 in the slots after; every channel of 0 to 31 appears exactly once; every owner holds 1 to 3 channels and some owner holds 3. `beam_order`: each beam appears once.
All inputs are finite; a program needn't handle non-finite values.
Results may differ from the reference program's by a relative error of at most 0.0038.
Values may be sent and summed in bfloat16 or wider, within the bound.
No kernel may reach another device: no remote copies, remote signals or barrier semaphores. Data moves between devices by JAX's collectives and lax.ppermute only.
A program may use at most 128 MiB of HBM per device.

```python
import math
import jax
import jax.numpy as jnp
from jax import lax

F = 2048
NFFT = 2048
TAPS = 4
BEAMS = 1024
MOST = 3
NFR = 192
NSAMP = 393216
NCH = 32
SLOTS = 48
N_FEED = 8


def draw_allocation(key, part):
    key = jax.random.fold_in(key, 11)
    owners = SLOTS // MOST
    key_heavy, key_order, key_channels = jax.random.split(key, 3)
    heavy = jax.random.randint(key_heavy, (), 1, owners // 2 + 1)
    owner_order = jax.random.permutation(key_order, owners)
    ranking = jnp.argsort(owner_order)
    counts = jnp.where(ranking < heavy, MOST, jnp.where(ranking < 2 * heavy, MOST - 2, MOST - 1))
    starts = jnp.cumsum(counts) - counts
    shuffled = jax.random.permutation(key_channels, NCH)
    slot_index = jnp.arange(MOST)
    wanted = starts[:, None] + slot_index[None, :]
    chosen = shuffled[jnp.clip(wanted, 0, NCH - 1)]
    return jnp.where(slot_index[None, :] < counts[:, None], chosen, -1).astype(jnp.int32)


def block_levels(rng, shape, shards, low, high):
    level = 1.0
    for axis_at, shards_of in shards:
        heights = jax.random.uniform(jax.random.fold_in(jax.random.fold_in(rng, 6), axis_at), (shards_of,), jnp.float32, low / len(shards), high / len(shards))
        level = level * jnp.repeat(jnp.exp(heights), shape[axis_at] // shards_of).reshape((-1,) + (1,) * (len(shape) - 1 - axis_at))
    return level


def noise(own_key, shape, scale, most, cuts=(), kind=jnp.bfloat16):
    values = jax.random.normal(own_key, shape, jnp.float32) * scale
    if len(cuts) > 0:
        values = block_levels(own_key, shape, cuts, -0.22, 0.18) * values
    return jnp.clip(values, min=-most, max=most).astype(kind)


def setup_inputs(seed: int = 0) -> dict:
    key_list = jax.random.split(jax.random.key(seed), 5)
    volts = noise(key_list[0], (F, NSAMP), 1.0, 6.0, ((0, 8), (1, 16)))
    beam_weights = noise(key_list[1], (2, BEAMS, F), F ** -0.5, 0.125, ((2, 8),))
    allocation = draw_allocation(jax.random.fold_in(key_list[4], 71), 0)
    beam_order = jax.random.permutation(key_list[3], BEAMS).astype(jnp.int32)
    return dict(volts=volts, beam_weights=beam_weights, allocation=allocation, beam_order=beam_order)


def window_taps():
    length = TAPS * NFFT
    positions = jnp.arange(length, dtype=jnp.float32)
    centred = (positions - 0.5 * length + 0.5) / NFFT
    hann_taper = 0.5 - 0.5 * jnp.cos(2.0 * math.pi * (positions + 0.5) / length)
    coeffs = jnp.sinc(centred) * hann_taper
    coeffs = coeffs * jnp.sqrt(NFFT / jnp.sum(coeffs * coeffs))
    return coeffs.reshape(TAPS, NFFT)

def dft_rows(channels):
    bin_index = jnp.arange(channels, dtype=jnp.int32)
    sample_index = jnp.arange(NFFT, dtype=jnp.int32)
    angles = (bin_index[:, None] * sample_index[None, :] % NFFT).astype(jnp.float32) * (2.0 * math.pi / NFFT)
    rows_both = jnp.stack([jnp.cos(angles), -jnp.sin(angles)], axis=1) / math.sqrt(NFFT)
    return rows_both.reshape(2 * channels, NFFT)

def reference(volts, beam_weights, allocation, beam_order):
    coeffs = window_taps()
    transform = dft_rows(NCH)
    blocks = volts.reshape(N_FEED, F // N_FEED, NFR, NFFT)

    def one_block(feed_block):
        rows_here = feed_block.shape[0]
        framed = jnp.concatenate([jnp.zeros((rows_here, TAPS - 1, NFFT), feed_block.dtype), feed_block], axis=1)
        summed = jnp.zeros((rows_here, NFR, NFFT), jnp.float32)
        for tap_index in range(TAPS):
            summed = summed + coeffs[tap_index] * framed[:, tap_index:tap_index + NFR].astype(jnp.float32)
        result = lax.dot_general(transform, summed, (((1,), (2,)), ((), ())), precision=lax.Precision.HIGHEST, preferred_element_type=jnp.float32)
        return result.astype(jnp.bfloat16).reshape(NCH, 2, rows_here, NFR)
    per_block = lax.map(one_block, blocks)
    spectra = jnp.transpose(per_block, (1, 2, 4, 0, 3)).reshape(NCH, 2, NFR, F)
    slot_list = allocation.reshape(SLOTS)
    is_live = slot_list >= 0
    safe_list = jnp.clip(slot_list, 0, NCH - 1).astype(jnp.int32)
    chosen = jnp.take(spectra, safe_list, axis=0) * is_live[:, None, None, None].astype(jnp.bfloat16)

    def one_slot(slot_rows):
        values = slot_rows.astype(jnp.float32)
        turned = jnp.stack([values[1], -values[0]])
        real_part = jnp.einsum('ctf,ctg->fg', values, values, precision=lax.Precision.HIGHEST)
        imag_part = jnp.einsum('ctf,ctg->fg', turned, values, precision=lax.Precision.HIGHEST)
        return jnp.stack([real_part, imag_part]) / NFR
    visibility = lax.map(one_slot, chosen)
    weights = jnp.take(beam_weights, beam_order, axis=1).astype(jnp.float32)

    def one_channel(channel):
        values = channel.astype(jnp.float32)
        hp = lax.Precision.HIGHEST
        real_part = jnp.einsum('bf,tf->bt', weights[0], values[0], precision=hp) - jnp.einsum('bf,tf->bt', weights[1], values[1], precision=hp)
        imag_part = jnp.einsum('bf,tf->bt', weights[0], values[1], precision=hp) + jnp.einsum('bf,tf->bt', weights[1], values[0], precision=hp)
        return lax.optimization_barrier(jnp.sum(real_part * real_part + imag_part * imag_part, axis=1)) / NFR
    beam_energy = lax.map(one_channel, spectra)
    slotted = jnp.take(beam_energy, safe_list, axis=0) * is_live[:, None].astype(jnp.float32)
    return (visibility, slotted.T)
```

```python
import functools
import math

import jax
import jax.numpy as jnp
import ml_dtypes
import numpy as np
from jax import lax
from jax.experimental import pallas as pl
from jax.experimental.pallas import tpu as pltpu
from jax.sharding import PartitionSpec as P

NFFT = 2048
TAPS = 4
VMEM = 48 * 1024 * 1024
NT = (((1,), (1,)), ((), ()))


def tap_transform(channels):
    length = TAPS * NFFT
    positions = np.arange(length, dtype=np.float64)
    coeffs = np.sinc((positions - 0.5 * length + 0.5) / NFFT)
    coeffs = coeffs * (0.5 - 0.5 * np.cos(2.0 * math.pi * (positions + 0.5) / length))
    coeffs = coeffs * np.sqrt(NFFT / np.sum(coeffs * coeffs))
    coeffs = coeffs.reshape(TAPS, NFFT)
    angles = (np.arange(channels)[:, None] * np.arange(NFFT)[None, :] % NFFT) * (2.0 * math.pi / NFFT)
    rows = np.stack([np.cos(angles), -np.sin(angles)], axis=1) / math.sqrt(NFFT)
    rows = rows.reshape(2 * channels, NFFT)
    full = (coeffs[:, None, :] * rows[None]).reshape(TAPS * 2 * channels, NFFT)
    high = full.astype(ml_dtypes.bfloat16)
    low = (full - high.astype(np.float64)).astype(ml_dtypes.bfloat16)
    return np.concatenate([high, low], axis=0)


def frame_products(table_ref, volts_ref, rows):
    product = lax.dot_general(
        table_ref[...], volts_ref[...], NT, preferred_element_type=jnp.float32
    )
    half = product.shape[0] // 2
    product = product[:half] + product[half:]
    return [product[tap * rows : (tap + 1) * rows] for tap in range(TAPS)]


def last_frames_kernel(table_ref, volts_ref, total_ref):
    step = pl.program_id(0)
    rows = total_ref.shape[1]

    @pl.when(step == 0)
    def _():
        total_ref[...] = jnp.zeros_like(total_ref)

    parts = frame_products(table_ref, volts_ref, rows)
    for tap in range(TAPS):
        at = step + TAPS - 1 - tap
        total_ref[at] = total_ref[at] + parts[tap]


def first_frames_kernel(table_ref, volts_ref, last_ref, target_ref, total_ref, select_ref):
    step = pl.program_id(0)
    rows = total_ref.shape[1]
    done = total_ref.shape[0] - (TAPS - 1)

    @pl.when(step == 0)
    def _():
        total_ref[:done] = jnp.zeros((done,) + total_ref.shape[1:], jnp.float32)
        total_ref[done:] = last_ref[...]

    parts = frame_products(table_ref, volts_ref, rows)
    for tap in range(TAPS):
        at = step + TAPS - 1 - tap
        total_ref[at] = total_ref[at] + parts[tap]
    place = lax.broadcasted_iota(jnp.int32, select_ref.shape, 1)
    select_ref[...] = jnp.where(place == target_ref[...], 1.0, 0.0).astype(jnp.bfloat16)


def choose_kernel(total_ref, carry_ref, select_ref, out_ref):
    ahead = carry_ref.shape[0]
    head = (total_ref[:ahead] + carry_ref[...]).astype(jnp.bfloat16)
    tail = total_ref[ahead:].astype(jnp.bfloat16)
    spectra = jnp.concatenate([head, tail], axis=0)
    out_ref[...] = jnp.dot(
        select_ref[...], spectra, preferred_element_type=jnp.float32
    ).astype(jnp.bfloat16)


def order_kernel(order_ref, weights_ref, out_ref):
    beams = weights_ref.shape[1]
    share = out_ref.shape[2]
    place = lax.broadcasted_iota(jnp.int32, (share, beams), 1)
    hot = jnp.where(place == order_ref[...], 1.0, 0.0).astype(jnp.bfloat16)
    for part in range(2):
        out_ref[0, part] = jnp.dot(
            hot, weights_ref[part], preferred_element_type=jnp.float32
        ).astype(jnp.bfloat16)


def swap_parts(values, half, sign):
    lanes = values.shape[1]
    lane = lax.broadcasted_iota(jnp.int32, values.shape, 1)
    ahead = pltpu.roll(values, lanes - half, 1)
    behind = pltpu.roll(values, half, 1)
    return jnp.where(lane % (2 * half) < half, sign * ahead, -sign * behind)


def pair_kernel(first, final, half, scale, where_ref, *refs):
    refs = list(refs)
    if first:
        own_ref, other_ref, weight_a_ref, weight_b_ref = refs[:4]
        vis_ref, left_ref, voltage_ref = refs[4:7]
        own = own_ref[0].astype(jnp.float32).T
        left = jnp.concatenate([own, swap_parts(own, half, 1.0)], axis=0).astype(jnp.bfloat16)
        left_ref[0] = left
    else:
        own_ref, other_ref, weight_a_ref, weight_b_ref, left_ref, before_ref, _ = refs[:7]
        vis_ref = refs[7]
        left = left_ref[0]
    core = where_ref[1]
    width = own_ref.shape[2]
    voltage = None
    for ref, weight_ref, at in (
        (own_ref, weight_a_ref, core),
        (other_ref, weight_b_ref, 1 - core),
    ):
        product = jnp.dot(left, ref[0], preferred_element_type=jnp.float32) * scale
        columns = pl.ds(pl.multiple_of(at * width, width), width)
        vis_ref[0, 0, :, columns] = product[: product.shape[0] // 2]
        vis_ref[0, 1, :, columns] = product[product.shape[0] // 2 :]
        beams = weight_ref.shape[1] * weight_ref.shape[2]
        term = lax.dot_general(
            weight_ref[0].reshape(beams, width), ref[0], NT, preferred_element_type=jnp.float32
        )
        voltage = term if voltage is None else voltage + term
    if first:
        voltage_ref[0] = voltage
        return
    voltage = voltage + before_ref[0]
    if not final:
        refs[8][0] = voltage
        return
    power_ref = refs[8]
    share = voltage.shape[0] // 2
    beam = voltage[:share] - swap_parts(voltage[share:], half, 1.0)
    power = jnp.sum(beam * beam, axis=1, keepdims=True) * scale
    slot = lax.broadcasted_iota(jnp.int32, power_ref.shape, 1)
    power_ref[...] = jnp.where(slot == pl.program_id(0), power, power_ref[...])


def params():
    return pltpu.CompilerParams(vmem_limit_bytes=VMEM)


def pair_call(kind, half, scale, where, own, other, weights, left=None, voltage=None, vis=None):
    slots, rows, width = own.shape
    devices, parts, share, _ = weights.shape
    block = lambda shape, at: pl.BlockSpec(shape, at)
    per_slot = lambda *shape: block((1,) + shape, lambda s, w: (s,) + (0,) * len(shape))
    in_specs = [
        per_slot(rows, width),
        per_slot(rows, width),
        block((1, parts, share, width), lambda s, w: (2 * w[0] + w[1], 0, 0, 0)),
        block((1, parts, share, width), lambda s, w: (2 * w[0] + 1 - w[1], 0, 0, 0)),
    ]
    args = [own, other, weights, weights]
    vis_shape = jax.ShapeDtypeStruct((slots, 2, width, devices * width), jnp.float32)
    vis_spec = block((1, 2, width, 2 * width), lambda s, w: (s, 0, 0, w[0]))
    voltage_shape = jax.ShapeDtypeStruct((slots, parts * share, rows), jnp.float32)
    left_shape = jax.ShapeDtypeStruct((slots, 2 * width, rows), jnp.bfloat16)
    power_shape = jax.ShapeDtypeStruct((share, slots), jnp.float32)
    aliases = {}
    if kind == "first":
        out_shape = [vis_shape, left_shape, voltage_shape]
        out_specs = [vis_spec, per_slot(2 * width, rows), per_slot(parts * share, rows)]
    else:
        in_specs += [
            per_slot(2 * width, rows),
            per_slot(parts * share, rows),
            pl.BlockSpec(memory_space=pl.ANY),
        ]
        args += [left, voltage, vis]
        aliases = {7: 0}
        if kind == "final":
            out_shape = [vis_shape, power_shape]
            out_specs = [vis_spec, block((share, slots), lambda s, w: (0, 0))]
        else:
            out_shape = [vis_shape, voltage_shape]
            out_specs = [vis_spec, per_slot(parts * share, rows)]
    flops = 2 * slots * rows * width * 2 * (2 * width + parts * share)
    moved = slots * 2 * width * 2 * width * 4 + 6 * slots * rows * width
    return pl.pallas_call(
        functools.partial(pair_kernel, kind == "first", kind == "final", half, scale),
        out_shape=out_shape,
        grid_spec=pltpu.PrefetchScalarGridSpec(
            num_scalar_prefetch=1, grid=(slots,), in_specs=in_specs, out_specs=out_specs
        ),
        input_output_aliases=aliases,
        compiler_params=params(),
        cost_estimate=pl.CostEstimate(flops=flops, bytes_accessed=moved, transcendentals=0),
    )(where, *args)


def shards(volts, beam_weights, allocation, beam_order):
    feeds_dev = volts.shape[0]
    frames_dev = volts.shape[1] // NFFT
    owners = lax.axis_size("freq")
    devices = lax.axis_size("feed")
    total_frames = frames_dev * owners
    slots_dev = allocation.shape[1]
    channels = (slots_dev - 1) * allocation.shape[0]
    rows = 2 * channels
    late = TAPS - 1
    early = frames_dev - late
    beams = beam_weights.shape[1]
    share = beams // devices
    f32, bf16 = jnp.float32, jnp.bfloat16
    table = jnp.asarray(tap_transform(channels))
    table_spec = pl.BlockSpec(table.shape, lambda i: (0, 0))
    frame_flops = 2 * table.shape[0] * feeds_dev * NFFT

    last = pl.pallas_call(
        last_frames_kernel,
        out_shape=jax.ShapeDtypeStruct((2 * late, rows, feeds_dev), f32),
        grid=(late,),
        in_specs=[table_spec, pl.BlockSpec((feeds_dev, NFFT), lambda i: (0, early + i))],
        out_specs=pl.BlockSpec((2 * late, rows, feeds_dev), lambda i: (0, 0, 0)),
        compiler_params=params(),
        cost_estimate=pl.CostEstimate(
            flops=late * frame_flops, bytes_accessed=late * feeds_dev * NFFT * 2, transcendentals=0
        ),
    )(table, volts)
    carry = lax.ppermute(last[late:], "freq", [(i, i + 1) for i in range(owners - 1)])

    ordered = pl.pallas_call(
        order_kernel,
        out_shape=jax.ShapeDtypeStruct((devices, 2, share, feeds_dev), bf16),
        grid=(devices,),
        in_specs=[
            pl.BlockSpec((share, 1), lambda i: (i, 0)),
            pl.BlockSpec(beam_weights.shape, lambda i: (0, 0, 0)),
        ],
        out_specs=pl.BlockSpec((1, 2, share, feeds_dev), lambda i: (i, 0, 0, 0)),
        compiler_params=params(),
        cost_estimate=pl.CostEstimate(
            flops=4 * beams * beams * feeds_dev, bytes_accessed=4 * beams * feeds_dev, transcendentals=0
        ),
    )(beam_order.reshape(beams, 1), beam_weights)
    weights = lax.all_to_all(ordered, "feed", split_axis=0, concat_axis=0, tiled=True)

    slot_list = allocation.reshape(-1)
    slots = slot_list.shape[0]
    chosen_rows = slots * 2 * frames_dev
    target = (
        jnp.arange(frames_dev, dtype=jnp.int32)[None, None, :] * rows
        + jnp.arange(2, dtype=jnp.int32)[None, :, None]
        + 2 * slot_list[:, None, None]
    )
    target = jnp.where(slot_list[:, None, None] >= 0, target, -1).reshape(chosen_rows, 1)
    per_step = chosen_rows // early
    total, select = pl.pallas_call(
        first_frames_kernel,
        out_shape=[
            jax.ShapeDtypeStruct((frames_dev, rows, feeds_dev), f32),
            jax.ShapeDtypeStruct((chosen_rows, frames_dev * rows), bf16),
        ],
        grid=(early,),
        in_specs=[
            table_spec,
            pl.BlockSpec((feeds_dev, NFFT), lambda i: (0, i)),
            pl.BlockSpec((late, rows, feeds_dev), lambda i: (0, 0, 0)),
            pl.BlockSpec((per_step, 1), lambda i: (i, 0)),
        ],
        out_specs=[
            pl.BlockSpec((frames_dev, rows, feeds_dev), lambda i: (0, 0, 0)),
            pl.BlockSpec((per_step, frames_dev * rows), lambda i: (i, 0)),
        ],
        compiler_params=params(),
        cost_estimate=pl.CostEstimate(
            flops=early * frame_flops, bytes_accessed=early * feeds_dev * NFFT * 2, transcendentals=0
        ),
    )(table, volts, last, target)

    outgoing = pl.pallas_call(
        choose_kernel,
        out_shape=jax.ShapeDtypeStruct((chosen_rows, feeds_dev), bf16),
        compiler_params=params(),
    )(
        total.reshape(frames_dev * rows, feeds_dev), carry.reshape(late * rows, feeds_dev), select
    )
    received = lax.all_to_all(
        outgoing.reshape(owners, slots_dev, 2 * frames_dev, feeds_dev),
        "freq",
        split_axis=0,
        concat_axis=0,
        tiled=True,
    )
    own = received.transpose(1, 0, 2, 3).reshape(slots_dev, 2 * total_frames, feeds_dev)

    def moved(x, by):
        return lax.ppermute(x, "feed", [(i, (i + by) % devices) for i in range(devices)])

    def swapped(x):
        return lax.ppermute(x, "feed", [(i, i ^ 1) for i in range(devices)])

    me = lax.axis_index("feed").astype(jnp.int32)
    chips = devices // 2
    place = lambda behind: jnp.stack([(me // 2 - behind) % chips, me % 2])
    call = functools.partial(pair_call, half=frames_dev, scale=1.0 / total_frames)
    sibling = swapped(own)
    blocks = [moved(own, 2), moved(own, -2), moved(own, 4)]
    others = [swapped(x) for x in blocks]
    vis, left, voltage = call("first", where=place(0), own=own, other=sibling, weights=weights)
    for behind, x, y in ((1, blocks[0], others[0]), (-1, blocks[1], others[1])):
        vis, voltage = call(
            "middle", where=place(behind), own=x, other=y, weights=weights,
            left=left, voltage=voltage, vis=vis,
        )
    vis, power = call(
        "final", where=place(2), own=blocks[2], other=others[2], weights=weights,
        left=left, voltage=voltage, vis=vis,
    )
    return (vis, power)


def solution(mesh):
    in_specs = (P("feed", "freq"), P(None, None, "feed"), P(), P())
    out_specs = (P("freq", None, "feed", None), P("feed", "freq"))
    return jax.shard_map(shards, mesh=mesh, in_specs=in_specs, out_specs=out_specs, check_vma=False)
```

```python
import functools
import math

import jax
import jax.numpy as jnp
import ml_dtypes
import numpy as np
from jax import lax
from jax.experimental import pallas as pl
from jax.experimental.pallas import tpu as pltpu
from jax.sharding import PartitionSpec as P

NFFT = 2048
TAPS = 4
AHEAD = 2
COST = {"middle": pl.CostEstimate(flops=1, bytes_accessed=1, transcendentals=0)}
WIDE_VMEM = 62 * 1024 * 1024
NT = (((1,), (1,)), ((), ()))


def tap_transform(channels):
    length = TAPS * NFFT
    positions = np.arange(length, dtype=np.float64)
    coeffs = np.sinc((positions - 0.5 * length + 0.5) / NFFT)
    coeffs = coeffs * (0.5 - 0.5 * np.cos(2.0 * math.pi * (positions + 0.5) / length))
    coeffs = coeffs * np.sqrt(NFFT / np.sum(coeffs * coeffs))
    coeffs = coeffs.reshape(TAPS, NFFT)
    angles = (np.arange(channels)[:, None] * np.arange(NFFT)[None, :] % NFFT) * (2.0 * math.pi / NFFT)
    rows = np.stack([np.cos(angles), -np.sin(angles)], axis=1) / math.sqrt(NFFT)
    rows = rows.reshape(2 * channels, NFFT)
    full = (coeffs[:, None, :] * rows[None]).reshape(TAPS * 2 * channels, NFFT)
    high = full.astype(ml_dtypes.bfloat16)
    low = (full - high.astype(np.float64)).astype(ml_dtypes.bfloat16)
    return np.concatenate([high, low], axis=0)


def frame_loop(table_hbm, volts_hbm, table, frames, table_sem, frame_sems, total_ref, first, extra):
    count = frames.shape[0]
    rows = total_ref.shape[1]

    def table_copy():
        return pltpu.make_async_copy(table_hbm, table, table_sem)

    def frame_copy(i):
        at = pl.multiple_of((first + i) * NFFT, NFFT)
        return pltpu.make_async_copy(
            volts_hbm.at[:, pl.ds(at, NFFT)], frames.at[i], frame_sems.at[i]
        )

    table_copy().start()
    for i in range(AHEAD):
        frame_copy(i).start()
    extra(0)
    table_copy().wait()

    def step(i, _):
        @pl.when(i + AHEAD < count)
        def _():
            frame_copy(i + AHEAD).start()

        frame_copy(i).wait()
        product = lax.dot_general(
            table[...], frames[i], NT, preferred_element_type=jnp.float32
        )
        half = product.shape[0] // 2
        product = product[:half] + product[half:]
        for tap in range(TAPS):
            at = i + TAPS - 1 - tap
            total_ref[at] = total_ref[at] + product[tap * rows : (tap + 1) * rows]
        extra(i)
        return 0

    lax.fori_loop(0, count, step, 0)


def last_frames_kernel(
    first, table_hbm, volts_hbm, own_ref, next_ref, total, table, frames, table_sem, frame_sems
):
    total[...] = jnp.zeros_like(total)
    frame_loop(
        table_hbm, volts_hbm, table, frames, table_sem, frame_sems, total, first, lambda i: None
    )
    own_ref[...] = total[: TAPS - 1]
    next_ref[...] = total[TAPS - 1 :]


def first_frames_kernel(
    allocation_hbm, table_hbm, volts_hbm, last_ref, carry_ref, out_ref,
    total, hot, spectra, allocation_ref, allocation_sem, table, frames, table_sem, frame_sems,
):
    allocation_copy = pltpu.make_async_copy(allocation_hbm, allocation_ref, allocation_sem)
    allocation_copy.start()
    count, rows, width = total.shape
    slots, owners = allocation_ref.shape
    late = last_ref.shape[0]
    done = count - late
    total[:late] = carry_ref[...]
    total[late:done] = jnp.zeros((done - late, rows, width), jnp.float32)
    total[done:] = last_ref[...]
    size = 2 * count
    group = 2 * slots * size
    shape = (size, count * rows)
    row = lax.broadcasted_iota(jnp.int32, shape, 0)
    part = (row >= count).astype(jnp.int32)
    offset = lax.broadcasted_iota(jnp.int32, shape, 1) - (row - part * count) * rows - part

    allocation_copy.wait()

    def choose(i):
        pair = jnp.minimum(i, owners // 2 - 1)
        chosen = []
        for owner in range(2):
            for slot in range(slots):
                channel = allocation_ref[slot, 2 * pair + owner]
                wanted = jnp.where(channel >= 0, 2 * channel, -2 * count * rows)
                chosen.append(jnp.where(offset == wanted, 1.0, 0.0))
        hot[pl.ds(pl.multiple_of(pair * group, group), group)] = jnp.concatenate(
            chosen, axis=0
        ).astype(jnp.bfloat16)

    frame_loop(
        table_hbm, volts_hbm, table, frames, table_sem, frame_sems, total, 0, choose
    )
    for t in range(count):
        spectra[pl.ds(t * rows, rows)] = total[t].astype(jnp.bfloat16)

    def write(i, _):
        at = pl.ds(pl.multiple_of(i * 4 * group, 4 * group), 4 * group)
        out_ref[at] = jnp.dot(hot[at], spectra[...], preferred_element_type=jnp.float32).astype(
            jnp.bfloat16
        )
        return 0

    lax.fori_loop(0, owners // 8, write, 0)


def filter_scratch(table, feeds, count):
    return [
        pltpu.VMEM(table.shape, jnp.bfloat16),
        pltpu.VMEM((count, feeds, NFFT), jnp.bfloat16),
        pltpu.SemaphoreType.DMA,
        pltpu.SemaphoreType.DMA((count,)),
    ]


def order_kernel(order_ref, weights_ref, *out_refs):
    beams = weights_ref.shape[1]
    devices, share = order_ref.shape
    chips = len(out_refs)
    me = lax.axis_index("feed")
    chip, core = me // 2, me % 2
    numbers = order_ref[...].astype(jnp.float32).T
    of_device = lax.broadcasted_iota(jnp.int32, numbers.shape, 1)
    place = lax.broadcasted_iota(jnp.int32, (share, beams), 1)
    for ahead, out_ref in enumerate(out_refs):
        to = lax.rem(chip + ahead, chips)
        hot = []
        for other in range(2):
            device = 2 * to + (core if other == 0 else 1 - core)
            wanted = jnp.sum(jnp.where(of_device == device, numbers, 0.0), axis=1, keepdims=True)
            hot.append(jnp.where(place == wanted.astype(jnp.int32), 1.0, 0.0).astype(jnp.bfloat16))
        hot = jnp.concatenate(hot, axis=0)
        for part in range(2):
            rows = jnp.dot(hot, weights_ref[part], preferred_element_type=jnp.float32)
            rows = rows.astype(jnp.bfloat16)
            out_ref[0, part] = rows[:share]
            out_ref[1, part] = rows[share:]


def swap_parts(values, half, axis):
    count = values.shape[axis]
    place = lax.broadcasted_iota(jnp.int32, values.shape, axis)
    ahead = pltpu.roll(values, count - half, axis)
    behind = pltpu.roll(values, half, axis)
    return jnp.where(place % (2 * half) < half, ahead, -behind)


def pair_kernel(behind, kind, half, scale, *refs):
    refs = list(refs)
    pairs = len(behind)
    block_refs = refs[: 4 * pairs]
    weight_refs = refs[4 * pairs : 6 * pairs]
    refs = refs[6 * pairs :]
    if kind == "first":
        vis_hbm, left_hbm, result_ref = refs[:3]
        refs = refs[3:]
    else:
        left_hbm, voltage_hbm, _, vis_hbm, result_ref = refs[:5]
        refs = refs[5:]
    values, weights, left, voltages, out, sems, weight_sems, out_sems, save_sems = refs
    slots, rows, narrow = values.shape[1:]
    width = 2 * narrow
    chips = vis_hbm.shape[3] // (2 * width)
    me = lax.axis_index("feed")
    chip, core = me // 2, me % 2

    def slot_copies(slot):
        copies = [(ref.at[slot], values.at[i, slot]) for i, ref in enumerate(block_refs)]
        if kind != "first":
            copies += [(left_hbm.at[slot], left.at[slot]), (voltage_hbm.at[slot], voltages.at[slot])]
        return [
            pltpu.make_async_copy(source, target, sems.at[slot, i])
            for i, (source, target) in enumerate(copies)
        ]

    weight_copies = [
        pltpu.make_async_copy(ref.at[0], weights.at[i], weight_sems.at[i])
        for i, ref in enumerate(weight_refs)
    ]

    def save_copies(slot):
        copies = []
        if kind != "last":
            copies.append((voltages.at[slot], result_ref.at[slot]))
        if kind == "first":
            copies.append((left.at[slot], left_hbm.at[slot]))
        return [
            pltpu.make_async_copy(source, target, save_sems.at[slot, i])
            for i, (source, target) in enumerate(copies)
        ]

    def out_copy(slot, pair):
        to = lax.rem(chip + chips - behind[pair], chips)
        at = pl.multiple_of(to * 2 * width, 2 * width)
        return pltpu.make_async_copy(
            out.at[slot, pair],
            vis_hbm.at[slot, :, :, pl.ds(at, 2 * width)],
            out_sems.at[slot, pair],
        )

    for copy in slot_copies(0) + weight_copies + slot_copies(1) + slot_copies(2):
        copy.start()

    def step(slot, _):
        for copy in slot_copies(slot):
            copy.wait()

        def value(i):
            return jnp.concatenate([values[2 * i, slot], values[2 * i + 1, slot]], axis=1)

        if kind == "first":
            own = value(0).astype(jnp.float32).T
            left[slot] = jnp.concatenate([own, swap_parts(own, half, 1)], axis=0).astype(
                jnp.bfloat16
            )
        for pair in range(pairs):
            for side, at in ((0, core), (1, 1 - core)):
                product = jnp.dot(
                    left[slot], value(2 * pair + side), preferred_element_type=jnp.float32
                )
                product = product * scale
                columns = pl.ds(pl.multiple_of(at * width, width), width)
                out[slot, pair, 0, :, columns] = product[:width]
                out[slot, pair, 1, :, columns] = product[width:]
            out_copy(slot, pair).start()

        @pl.when(slot == 0)
        def _():
            for copy in weight_copies:
                copy.wait()

        voltage = None
        for i in range(2 * pairs):
            weight = weights[i]
            weight = weight.reshape(weight.shape[0] * weight.shape[1], width)
            term = lax.dot_general(value(i), weight, NT, preferred_element_type=jnp.float32)
            voltage = term if voltage is None else voltage + term
        share = voltage.shape[1] // 2
        beam = voltage[:, :share] - swap_parts(voltage[:, share:], half, 0)
        if kind != "first":
            beam = voltages[slot] + beam
        if kind == "last":
            result_ref[pl.ds(slot, 1), :] = jnp.sum(beam * beam, axis=0, keepdims=True) * scale
        else:
            voltages[slot] = beam
            for copy in save_copies(slot):
                copy.start()
        return 0

    lax.fori_loop(0, slots, step, 0)
    for slot in range(slots):
        for pair in range(pairs):
            out_copy(slot, pair).wait()
        for copy in save_copies(slot):
            copy.wait()


def params():
    return pltpu.CompilerParams(vmem_limit_bytes=WIDE_VMEM)


def pair_call(
    kind, behind, half, scale, devices, blocks, weights, left=None, voltage=None, vis=None
):
    pairs = len(behind)
    slots, rows, narrow = blocks[0].shape
    width = 2 * narrow
    _, parts, share, _ = weights[0].shape
    anywhere = pl.BlockSpec(memory_space=pl.ANY)
    in_vmem = pl.BlockSpec(memory_space=pltpu.VMEM)
    args = list(blocks) + list(weights)
    vis_shape = jax.ShapeDtypeStruct((slots, 2, width, devices * width), jnp.float32)
    voltage_shape = jax.ShapeDtypeStruct((slots, rows, share), jnp.float32)
    left_shape = jax.ShapeDtypeStruct((slots, 2 * width, rows), jnp.bfloat16)
    power_shape = jax.ShapeDtypeStruct((slots, share), jnp.float32)
    aliases = {}
    if kind == "first":
        out_shape, out_specs = [vis_shape, left_shape, voltage_shape], [anywhere] * 3
    else:
        args += [left, voltage, vis]
        aliases = {len(args) - 1: 0}
        if kind == "middle":
            out_shape, out_specs = [vis_shape, voltage_shape], [anywhere] * 2
        else:
            out_shape, out_specs = [vis_shape, power_shape], [anywhere, in_vmem]
    flops = pairs * 4 * slots * rows * width * (2 * width + parts * share)
    moved = pairs * slots * 2 * width * 2 * width * 4 + 6 * slots * rows * width
    return pl.pallas_call(
        functools.partial(pair_kernel, behind, kind, half, scale),
        out_shape=out_shape,
        in_specs=[anywhere] * len(args),
        out_specs=out_specs,
        scratch_shapes=[
            pltpu.VMEM((4 * pairs, slots, rows, narrow), jnp.bfloat16),
            pltpu.VMEM((2 * pairs, parts, share, width), jnp.bfloat16),
            pltpu.VMEM(left_shape.shape, jnp.bfloat16),
            pltpu.VMEM(voltage_shape.shape, jnp.float32),
            pltpu.VMEM((slots, pairs, 2, width, 2 * width), jnp.float32),
            pltpu.SemaphoreType.DMA((slots, 4 * pairs + 2)),
            pltpu.SemaphoreType.DMA((2 * pairs,)),
            pltpu.SemaphoreType.DMA((slots, pairs)),
            pltpu.SemaphoreType.DMA((slots, 2)),
        ],
        input_output_aliases=aliases,
        compiler_params=params(),
        cost_estimate=COST.get(kind, pl.CostEstimate(flops=flops, bytes_accessed=moved, transcendentals=0)),
        name="pairs_" + kind,
    )(*args)


def shards(volts, beam_weights, allocation, beam_order):
    feeds_dev = volts.shape[0]
    frames_dev = volts.shape[1] // NFFT
    owners = lax.axis_size("freq")
    devices = lax.axis_size("feed")
    total_frames = frames_dev * owners
    slots_dev = allocation.shape[1]
    channels = (slots_dev - 1) * allocation.shape[0]
    rows = 2 * channels
    late = TAPS - 1
    early = frames_dev - late
    beams = beam_weights.shape[1]
    share = beams // devices
    f32, bf16 = jnp.float32, jnp.bfloat16
    table = jnp.asarray(tap_transform(channels))
    frame_flops = 2 * table.shape[0] * feeds_dev * NFFT
    anywhere = pl.BlockSpec(memory_space=pl.ANY)
    in_vmem = pl.BlockSpec(memory_space=pltpu.VMEM)

    def moved(x, by):
        return lax.ppermute(x, "feed", [(i, (i + by) % devices) for i in range(devices)])

    def swapped(x):
        return lax.ppermute(x, "feed", [(i, i ^ 1) for i in range(devices)])

    own_last, next_first = pl.pallas_call(
        functools.partial(last_frames_kernel, early),
        out_shape=[jax.ShapeDtypeStruct((late, rows, feeds_dev), f32)] * 2,
        in_specs=[anywhere, anywhere],
        out_specs=[in_vmem, in_vmem],
        scratch_shapes=[pltpu.VMEM((2 * late, rows, feeds_dev), f32)]
        + filter_scratch(table, feeds_dev, late),
        compiler_params=pltpu.CompilerParams(vmem_limit_bytes=WIDE_VMEM),
        cost_estimate=pl.CostEstimate(
            flops=late * frame_flops, bytes_accessed=late * feeds_dev * NFFT * 2, transcendentals=0
        ),
        name="last_frames",
    )(table, volts)
    carry = lax.ppermute(next_first, "freq", [(i, i + 1) for i in range(owners - 1)])
    ordered = pl.pallas_call(
        order_kernel,
        out_shape=[jax.ShapeDtypeStruct((2, 2, share, feeds_dev), bf16)] * (devices // 2),
        compiler_params=params(),
        cost_estimate=pl.CostEstimate(
            flops=4 * beams * beams * feeds_dev, bytes_accessed=4 * beams * feeds_dev, transcendentals=0
        ),
        name="order_beams",
    )(beam_order.reshape(devices, share), beam_weights)
    own_last, *ordered = lax.optimization_barrier((own_last, *ordered))
    weights = [ordered[0], moved(ordered[1], 2), moved(ordered[3], -2), moved(ordered[2], 4)]
    chosen_rows = owners * slots_dev * 2 * frames_dev
    outgoing = pl.pallas_call(
        first_frames_kernel,
        out_shape=jax.ShapeDtypeStruct((chosen_rows, feeds_dev), bf16),
        in_specs=[anywhere, anywhere, anywhere, in_vmem, in_vmem],
        out_specs=in_vmem,
        scratch_shapes=[
            pltpu.VMEM((frames_dev, rows, feeds_dev), f32),
            pltpu.VMEM((chosen_rows, frames_dev * rows), bf16),
            pltpu.VMEM((frames_dev * rows, feeds_dev), bf16),
            pltpu.SMEM((slots_dev, owners), jnp.int32),
            pltpu.SemaphoreType.DMA,
        ]
        + filter_scratch(table, feeds_dev, early),
        compiler_params=pltpu.CompilerParams(vmem_limit_bytes=WIDE_VMEM),
        cost_estimate=pl.CostEstimate(
            flops=early * frame_flops, bytes_accessed=early * feeds_dev * NFFT * 2, transcendentals=0
        ),
        name="first_frames",
    )(allocation.T, table, volts, own_last, carry)
    outgoing, weights[3] = lax.optimization_barrier((outgoing, weights[3]))
    received = lax.all_to_all(
        outgoing.reshape(owners, slots_dev, 2 * frames_dev, feeds_dev),
        "freq",
        split_axis=0,
        concat_axis=0,
        tiled=True,
    )

    received, weights[1], weights[2] = lax.optimization_barrier(
        (received, weights[1], weights[2])
    )
    weights_other = [swapped(x[1:]) for x in weights]
    by_chip = [[weights[d], weights_other[d]] for d in range(4)]

    own = received.transpose(1, 0, 2, 3).reshape(slots_dev, 2 * total_frames, feeds_dev)
    narrow = feeds_dev // 2
    own = [own[:, :, :narrow], own[:, :, narrow:]]
    up = [moved(own[0], 2)]
    down = [None, moved(own[1], -2)]
    up.append(moved(own[1], 2))
    down[0] = moved(own[0], -2)
    sibling = [swapped(x) for x in own]
    call = functools.partial(pair_call, half=frames_dev, scale=1.0 / total_frames, devices=devices)
    vis, left, voltage = call("first", (0,), blocks=own + sibling, weights=by_chip[0])
    up[0], down[1], voltage = lax.optimization_barrier((up[0], down[1], voltage))
    far = [moved(up[0], 2), moved(down[1], -2)]
    up_other = [swapped(x) for x in up]
    down_other = [swapped(x) for x in down]
    vis, voltage = call(
        "middle", (1, -1), blocks=up + up_other + down + down_other,
        weights=by_chip[1] + by_chip[2], left=left, voltage=voltage, vis=vis,
    )
    *far, voltage = lax.optimization_barrier((*far, voltage))
    far_other = [swapped(x) for x in far]
    vis, power = call(
        "last", (2,), blocks=far + far_other, weights=by_chip[3], left=left, voltage=voltage, vis=vis
    )
    return (vis, power.T)


def solution(mesh):
    in_specs = (P("feed", "freq"), P(None, None, "feed"), P(), P())
    out_specs = (P("freq", None, "feed", None), P("feed", "freq"))
    return jax.shard_map(shards, mesh=mesh, in_specs=in_specs, out_specs=out_specs, check_vma=False)
```

```python
import functools
import math

import jax
import jax.numpy as jnp
import ml_dtypes
import numpy as np
from jax import lax
from jax.experimental import pallas as pl
from jax.experimental.pallas import tpu as pltpu
from jax.sharding import PartitionSpec as P

NFFT = 2048
TAPS = 4
AHEAD = 2
WIDE_VMEM = 62 * 1024 * 1024
NT = (((1,), (1,)), ((), ()))


def tap_transform(channels):
    length = TAPS * NFFT
    positions = np.arange(length, dtype=np.float64)
    coeffs = np.sinc((positions - 0.5 * length + 0.5) / NFFT)
    coeffs = coeffs * (0.5 - 0.5 * np.cos(2.0 * math.pi * (positions + 0.5) / length))
    coeffs = coeffs * np.sqrt(NFFT / np.sum(coeffs * coeffs))
    coeffs = coeffs.reshape(TAPS, NFFT)
    angles = (np.arange(channels)[:, None] * np.arange(NFFT)[None, :] % NFFT) * (2.0 * math.pi / NFFT)
    rows = np.stack([np.cos(angles), -np.sin(angles)], axis=1) / math.sqrt(NFFT)
    rows = rows.reshape(2 * channels, NFFT)
    full = (coeffs[:, None, :] * rows[None]).reshape(TAPS * 2 * channels, NFFT)
    high = full.astype(ml_dtypes.bfloat16)
    low = (full - high.astype(np.float64)).astype(ml_dtypes.bfloat16)
    return high, low


def frame_loop(
    tables_hbm, volts_hbm, tables, frames, table_sems, frame_sems, total_ref, first, extra
):
    count = frames.shape[0]
    rows = total_ref.shape[1]

    table_copies = [
        pltpu.make_async_copy(source, target, table_sems.at[i])
        for i, (source, target) in enumerate(zip(tables_hbm, tables))
    ]
    high, low = tables

    def frame_copy(i):
        at = pl.multiple_of((first + i) * NFFT, NFFT)
        return pltpu.make_async_copy(
            volts_hbm.at[:, pl.ds(at, NFFT)], frames.at[i], frame_sems.at[i]
        )

    for copy in table_copies:
        copy.start()
    for i in range(AHEAD):
        frame_copy(i).start()
    extra(0)
    for copy in table_copies:
        copy.wait()

    def step(i, _):
        @pl.when(i + AHEAD < count)
        def _():
            frame_copy(i + AHEAD).start()

        frame_copy(i).wait()
        frame = frames[i]
        product = lax.dot_general(high[...], frame, NT, preferred_element_type=jnp.float32)
        product = product + lax.dot_general(
            low[...], frame, NT, preferred_element_type=jnp.float32
        )
        for tap in range(TAPS):
            at = i + TAPS - 1 - tap
            total_ref[at] = total_ref[at] + product[tap * rows : (tap + 1) * rows]
        extra(i)
        return 0

    lax.fori_loop(0, count, step, 0)


def last_frames_kernel(
    first, high_hbm, low_hbm, volts_hbm, own_ref, next_ref,
    total, high, low, frames, table_sems, frame_sems,
):
    total[...] = jnp.zeros_like(total)
    frame_loop(
        (high_hbm, low_hbm), volts_hbm, (high, low), frames, table_sems, frame_sems,
        total, first, lambda i: None,
    )
    own_ref[...] = total[: TAPS - 1]
    next_ref[...] = total[TAPS - 1 :]


def first_frames_kernel(
    allocation_hbm, high_hbm, low_hbm, volts_hbm, last_ref, carry_ref, out_ref,
    total, hot, spectra, allocation_ref, allocation_sem, high, low, frames, table_sems, frame_sems,
):
    allocation_copy = pltpu.make_async_copy(allocation_hbm, allocation_ref, allocation_sem)
    allocation_copy.start()
    count, rows, width = total.shape
    slots, owners = allocation_ref.shape
    late = last_ref.shape[0]
    done = count - late
    total[:late] = carry_ref[...]
    total[late:done] = jnp.zeros((done - late, rows, width), jnp.float32)
    total[done:] = last_ref[...]
    size = 2 * count
    group = 2 * slots * size
    shape = (size, count * rows)
    row = lax.broadcasted_iota(jnp.int32, shape, 0)
    part = (row >= count).astype(jnp.int32)
    offset = lax.broadcasted_iota(jnp.int32, shape, 1) - (row - part * count) * rows - part

    allocation_copy.wait()

    def choose(i):
        pair = jnp.minimum(i, owners // 2 - 1)
        chosen = []
        for owner in range(2):
            for slot in range(slots):
                channel = allocation_ref[slot, 2 * pair + owner]
                wanted = jnp.where(channel >= 0, 2 * channel, -2 * count * rows)
                chosen.append(jnp.where(offset == wanted, 1.0, 0.0))
        hot[pl.ds(pl.multiple_of(pair * group, group), group)] = jnp.concatenate(
            chosen, axis=0
        ).astype(jnp.bfloat16)

    frame_loop(
        (high_hbm, low_hbm), volts_hbm, (high, low), frames, table_sems, frame_sems,
        total, 0, choose,
    )
    for t in range(count):
        spectra[pl.ds(t * rows, rows)] = total[t].astype(jnp.bfloat16)

    def write(i, _):
        at = pl.ds(pl.multiple_of(i * 4 * group, 4 * group), 4 * group)
        out_ref[at] = jnp.dot(hot[at], spectra[...], preferred_element_type=jnp.float32).astype(
            jnp.bfloat16
        )
        return 0

    lax.fori_loop(0, owners // 8, write, 0)


def filter_scratch(tables, feeds, count):
    return [pltpu.VMEM(table.shape, table.dtype) for table in tables] + [
        pltpu.VMEM((count, feeds, NFFT), jnp.bfloat16),
        pltpu.SemaphoreType.DMA((2,)),
        pltpu.SemaphoreType.DMA((count,)),
    ]


def order_kernel(order_ref, weights_ref, *out_refs):
    beams = weights_ref.shape[1]
    devices, share = order_ref.shape
    chips = len(out_refs)
    me = lax.axis_index("feed")
    chip, core = me // 2, me % 2
    numbers = order_ref[...].astype(jnp.float32).T
    of_device = lax.broadcasted_iota(jnp.int32, numbers.shape, 1)
    place = lax.broadcasted_iota(jnp.int32, (share, beams), 1)
    for ahead, out_ref in enumerate(out_refs):
        to = lax.rem(chip + ahead, chips)
        hot = []
        for other in range(2):
            device = 2 * to + (core if other == 0 else 1 - core)
            wanted = jnp.sum(jnp.where(of_device == device, numbers, 0.0), axis=1, keepdims=True)
            hot.append(jnp.where(place == wanted.astype(jnp.int32), 1.0, 0.0).astype(jnp.bfloat16))
        hot = jnp.concatenate(hot, axis=0)
        for part in range(2):
            rows = jnp.dot(hot, weights_ref[part], preferred_element_type=jnp.float32)
            rows = rows.astype(jnp.bfloat16)
            out_ref[0, part] = rows[:share]
            out_ref[1, part] = rows[share:]


def swap_parts(values, half, axis):
    count = values.shape[axis]
    place = lax.broadcasted_iota(jnp.int32, values.shape, axis)
    ahead = pltpu.roll(values, count - half, axis)
    behind = pltpu.roll(values, half, axis)
    return jnp.where(place % (2 * half) < half, ahead, -behind)


def gather_kernel(behind, half, scale, *refs):
    refs = list(refs)
    pairs = len(behind)
    block_refs = refs[: 4 * pairs]
    weight_refs = refs[4 * pairs : 6 * pairs]
    vis_hbm, power_ref, values, weights, left, voltages, out, sems, weight_sems, out_sems = refs[
        6 * pairs :
    ]
    slots, rows, narrow = values.shape[2:]
    width = 2 * narrow
    chips = vis_hbm.shape[3] // (2 * width)
    me = lax.axis_index("feed")
    chip, core = me // 2, me % 2

    copies = []
    for pair in range(pairs):
        copies.append(
            [
                pltpu.make_async_copy(
                    block_refs[4 * pair + i], values.at[pair, i], sems.at[pair, i]
                )
                for i in range(4)
            ]
            + [
                pltpu.make_async_copy(
                    weight_refs[2 * pair + i].at[0], weights.at[pair, i], weight_sems.at[pair, i]
                )
                for i in range(2)
            ]
        )
        for copy in copies[pair]:
            copy.start()

    def out_copy(pair, slot):
        to = lax.rem(chip + chips - behind[pair], chips)
        at = pl.multiple_of(to * 2 * width, 2 * width)
        return pltpu.make_async_copy(
            out.at[pair, slot],
            vis_hbm.at[slot, :, :, pl.ds(at, 2 * width)],
            out_sems.at[pair, slot],
        )

    for pair in range(pairs):
        for copy in copies[pair]:
            copy.wait()
        for slot in range(slots):
            feeds = [
                jnp.concatenate([values[pair, 2 * i, slot], values[pair, 2 * i + 1, slot]], axis=1)
                for i in range(2)
            ]
            if pair == 0:
                own = feeds[0].astype(jnp.float32).T
                left[slot] = jnp.concatenate([own, swap_parts(own, half, 1)], axis=0).astype(
                    jnp.bfloat16
                )
            voltage = None if pair == 0 else voltages[slot]
            for side, at in ((0, core), (1, 1 - core)):
                product = (
                    jnp.dot(left[slot], feeds[side], preferred_element_type=jnp.float32) * scale
                )
                columns = pl.ds(pl.multiple_of(at * width, width), width)
                out[pair, slot, 0, :, columns] = product[:width]
                out[pair, slot, 1, :, columns] = product[width:]
                weight = weights[pair, side]
                weight = weight.reshape(weight.shape[0] * weight.shape[1], width)
                term = lax.dot_general(
                    feeds[side], weight, NT, preferred_element_type=jnp.float32
                )
                voltage = term if voltage is None else voltage + term
            out_copy(pair, slot).start()
            if pair < pairs - 1:
                voltages[slot] = voltage
            else:
                share = voltage.shape[1] // 2
                beam = voltage[:, :share] - swap_parts(voltage[:, share:], half, 0)
                power_ref[pl.ds(slot, 1), :] = jnp.sum(beam * beam, axis=0, keepdims=True) * scale
    for pair in range(pairs):
        for slot in range(slots):
            out_copy(pair, slot).wait()


def params():
    return pltpu.CompilerParams(vmem_limit_bytes=WIDE_VMEM)


def gather_call(behind, half, scale, devices, blocks, weights):
    pairs = len(behind)
    slots, rows, narrow = blocks[0].shape
    width = 2 * narrow
    _, parts, share, _ = weights[0].shape
    anywhere = pl.BlockSpec(memory_space=pl.ANY)
    args = list(blocks) + list(weights)
    flops = pairs * 4 * slots * rows * width * (2 * width + parts * share)
    moved = pairs * slots * 2 * width * 2 * width * 4 + 6 * slots * rows * width
    return pl.pallas_call(
        functools.partial(gather_kernel, behind, half, scale),
        out_shape=[
            jax.ShapeDtypeStruct((slots, 2, width, devices * width), jnp.float32),
            jax.ShapeDtypeStruct((slots, share), jnp.float32),
        ],
        in_specs=[anywhere] * len(args),
        out_specs=[anywhere, pl.BlockSpec(memory_space=pltpu.VMEM)],
        scratch_shapes=[
            pltpu.VMEM((pairs, 4, slots, rows, narrow), jnp.bfloat16),
            pltpu.VMEM((pairs, 2, parts, share, width), jnp.bfloat16),
            pltpu.VMEM((slots, 2 * width, rows), jnp.bfloat16),
            pltpu.VMEM((slots, rows, parts * share), jnp.float32),
            pltpu.VMEM((pairs, slots, 2, width, 2 * width), jnp.float32),
            pltpu.SemaphoreType.DMA((pairs, 4)),
            pltpu.SemaphoreType.DMA((pairs, 2)),
            pltpu.SemaphoreType.DMA((pairs, slots)),
        ],
        compiler_params=params(),
        cost_estimate=pl.CostEstimate(flops=flops, bytes_accessed=moved, transcendentals=0),
        name="gathered",
    )(*args)


def shards(volts, beam_weights, allocation, beam_order):
    feeds_dev = volts.shape[0]
    frames_dev = volts.shape[1] // NFFT
    owners = lax.axis_size("freq")
    devices = lax.axis_size("feed")
    total_frames = frames_dev * owners
    slots_dev = allocation.shape[1]
    channels = (slots_dev - 1) * allocation.shape[0]
    rows = 2 * channels
    late = TAPS - 1
    early = frames_dev - late
    beams = beam_weights.shape[1]
    share = beams // devices
    f32, bf16 = jnp.float32, jnp.bfloat16
    tables = [jnp.asarray(x) for x in tap_transform(channels)]
    frame_flops = 4 * tables[0].shape[0] * feeds_dev * NFFT
    anywhere = pl.BlockSpec(memory_space=pl.ANY)
    in_vmem = pl.BlockSpec(memory_space=pltpu.VMEM)

    def moved(x, by):
        return lax.ppermute(x, "feed", [(i, (i + by) % devices) for i in range(devices)])

    def swapped(x):
        return lax.ppermute(x, "feed", [(i, i ^ 1) for i in range(devices)])

    own_last, next_first = pl.pallas_call(
        functools.partial(last_frames_kernel, early),
        out_shape=[jax.ShapeDtypeStruct((late, rows, feeds_dev), f32)] * 2,
        in_specs=[anywhere] * 3,
        out_specs=[in_vmem, in_vmem],
        scratch_shapes=[pltpu.VMEM((2 * late, rows, feeds_dev), f32)]
        + filter_scratch(tables, feeds_dev, late),
        compiler_params=pltpu.CompilerParams(vmem_limit_bytes=WIDE_VMEM),
        cost_estimate=pl.CostEstimate(
            flops=late * frame_flops, bytes_accessed=late * feeds_dev * NFFT * 2, transcendentals=0
        ),
        name="last_frames",
    )(*tables, volts)
    carry = lax.ppermute(next_first, "freq", [(i, i + 1) for i in range(owners - 1)])
    ordered = pl.pallas_call(
        order_kernel,
        out_shape=[jax.ShapeDtypeStruct((2, 2, share, feeds_dev), bf16)] * (devices // 2),
        compiler_params=params(),
        cost_estimate=pl.CostEstimate(
            flops=4 * beams * beams * feeds_dev, bytes_accessed=4 * beams * feeds_dev, transcendentals=0
        ),
        name="order_beams",
    )(beam_order.reshape(devices, share), beam_weights)
    own_last, *ordered = lax.optimization_barrier((own_last, *ordered))
    weights = [ordered[0], moved(ordered[1], 2), moved(ordered[3], -2), moved(ordered[2], 4)]
    chosen_rows = owners * slots_dev * 2 * frames_dev
    outgoing = pl.pallas_call(
        first_frames_kernel,
        out_shape=jax.ShapeDtypeStruct((chosen_rows, feeds_dev), bf16),
        in_specs=[anywhere] * 4 + [in_vmem] * 2,
        out_specs=in_vmem,
        scratch_shapes=[
            pltpu.VMEM((frames_dev, rows, feeds_dev), f32),
            pltpu.VMEM((chosen_rows, frames_dev * rows), bf16),
            pltpu.VMEM((frames_dev * rows, feeds_dev), bf16),
            pltpu.SMEM((slots_dev, owners), jnp.int32),
            pltpu.SemaphoreType.DMA,
        ]
        + filter_scratch(tables, feeds_dev, early),
        compiler_params=pltpu.CompilerParams(vmem_limit_bytes=WIDE_VMEM),
        cost_estimate=pl.CostEstimate(
            flops=early * frame_flops, bytes_accessed=early * feeds_dev * NFFT * 2, transcendentals=0
        ),
        name="first_frames",
    )(allocation.T, *tables, volts, own_last, carry)
    outgoing, weights[3] = lax.optimization_barrier((outgoing, weights[3]))
    received = lax.all_to_all(
        outgoing.reshape(owners, slots_dev, 2 * frames_dev, feeds_dev),
        "freq",
        split_axis=0,
        concat_axis=0,
        tiled=True,
    )

    weights_other = [swapped(weights[0][1:]), None, None, swapped(weights[3][1:])]
    received, weights[1], weights[2], weights_other[0], weights_other[3] = lax.optimization_barrier(
        (received, weights[1], weights[2], weights_other[0], weights_other[3])
    )

    own = received.transpose(1, 0, 2, 3).reshape(slots_dev, 2 * total_frames, feeds_dev)
    narrow = feeds_dev // 2
    own = [own[:, :, :narrow], own[:, :, narrow:]]
    up = [moved(own[0], 2)]
    down = [None, moved(own[1], -2)]
    up.append(moved(own[1], 2))
    down[0] = moved(own[0], -2)
    far = [moved(up[0], 2), moved(down[1], -2)]
    sibling = [swapped(x) for x in own]
    up_other = [swapped(x) for x in up]
    down_other = [swapped(x) for x in down]
    weights_other[1:3] = [swapped(x[1:]) for x in weights[1:3]]
    far_other = [swapped(x) for x in far]
    by_chip = [[weights[d], weights_other[d]] for d in range(4)]
    vis, power = gather_call(
        (0, 1, -1, 2),
        half=frames_dev,
        scale=1.0 / total_frames,
        devices=devices,
        blocks=own + sibling + up + up_other + down + down_other + far + far_other,
        weights=[x for d in range(4) for x in by_chip[d]],
    )
    return (vis, power.T)


def solution(mesh):
    in_specs = (P("feed", "freq"), P(None, None, "feed"), P(), P())
    out_specs = (P("freq", None, "feed", None), P("feed", "freq"))
    return jax.shard_map(shards, mesh=mesh, in_specs=in_specs, out_specs=out_specs, check_vma=False)
```

```python
import functools
import math

import jax
import jax.numpy as jnp
import ml_dtypes
import numpy as np
from jax import lax
from jax.experimental import pallas as pl
from jax.experimental.pallas import tpu as pltpu
from jax.sharding import PartitionSpec as P

NFFT = 2048
TAPS = 4
AHEAD = 2
WIDE_VMEM = 62 * 1024 * 1024
NT = (((1,), (1,)), ((), ()))


def tap_transform(channels):
    length = TAPS * NFFT
    positions = np.arange(length, dtype=np.float64)
    coeffs = np.sinc((positions - 0.5 * length + 0.5) / NFFT)
    coeffs = coeffs * (0.5 - 0.5 * np.cos(2.0 * math.pi * (positions + 0.5) / length))
    coeffs = coeffs * np.sqrt(NFFT / np.sum(coeffs * coeffs))
    coeffs = coeffs.reshape(TAPS, NFFT)
    angles = (np.arange(channels)[:, None] * np.arange(NFFT)[None, :] % NFFT) * (2.0 * math.pi / NFFT)
    rows = np.stack([np.cos(angles), -np.sin(angles)], axis=1) / math.sqrt(NFFT)
    rows = rows.reshape(2 * channels, NFFT)
    full = (coeffs[:, None, :] * rows[None]).reshape(TAPS * 2 * channels, NFFT)
    high = full.astype(ml_dtypes.bfloat16)
    low = (full - high.astype(np.float64)).astype(ml_dtypes.bfloat16)
    return high, low


def frame_loop(
    tables_hbm, volts_hbm, tables, frames, table_sems, frame_sems, total_ref, first, extra
):
    count = frames.shape[0]
    rows = total_ref.shape[1]

    table_copies = [
        pltpu.make_async_copy(source, target, table_sems.at[i])
        for i, (source, target) in enumerate(zip(tables_hbm, tables))
    ]
    high, low = tables

    def frame_copy(i):
        at = pl.multiple_of((first + i) * NFFT, NFFT)
        return pltpu.make_async_copy(
            volts_hbm.at[:, pl.ds(at, NFFT)], frames.at[i], frame_sems.at[i]
        )

    for copy in table_copies:
        copy.start()
    for i in range(AHEAD):
        frame_copy(i).start()
    extra(0)
    for copy in table_copies:
        copy.wait()

    def step(i, _):
        @pl.when(i + AHEAD < count)
        def _():
            frame_copy(i + AHEAD).start()

        frame_copy(i).wait()
        frame = frames[i]
        product = lax.dot_general(high[...], frame, NT, preferred_element_type=jnp.float32)
        product = product + lax.dot_general(
            low[...], frame, NT, preferred_element_type=jnp.float32
        )
        for tap in range(TAPS):
            at = i + TAPS - 1 - tap
            total_ref[at] = total_ref[at] + product[tap * rows : (tap + 1) * rows]
        extra(i)
        return 0

    lax.fori_loop(0, count, step, 0)


def last_frames_kernel(
    first, high_hbm, low_hbm, volts_hbm, own_ref, next_ref,
    total, high, low, frames, table_sems, frame_sems,
):
    total[...] = jnp.zeros_like(total)
    frame_loop(
        (high_hbm, low_hbm), volts_hbm, (high, low), frames, table_sems, frame_sems,
        total, first, lambda i: None,
    )
    own_ref[...] = total[: TAPS - 1]
    next_ref[...] = total[TAPS - 1 :]


def first_frames_kernel(
    allocation_hbm, high_hbm, low_hbm, volts_hbm, last_ref, carry_ref, out_ref,
    total, hot, spectra, allocation_ref, allocation_sem, high, low, frames, table_sems, frame_sems,
):
    allocation_copy = pltpu.make_async_copy(allocation_hbm, allocation_ref, allocation_sem)
    allocation_copy.start()
    count, rows, width = total.shape
    slots, owners = allocation_ref.shape
    late = last_ref.shape[0]
    done = count - late
    total[:late] = carry_ref[...]
    total[late:done] = jnp.zeros((done - late, rows, width), jnp.float32)
    total[done:] = last_ref[...]
    size = 2 * count
    group = 2 * slots * size
    shape = (size, count * rows)
    row = lax.broadcasted_iota(jnp.int32, shape, 0)
    part = (row >= count).astype(jnp.int32)
    offset = lax.broadcasted_iota(jnp.int32, shape, 1) - (row - part * count) * rows - part

    allocation_copy.wait()

    def choose(i):
        pair = jnp.minimum(i, owners // 2 - 1)
        chosen = []
        for owner in range(2):
            for slot in range(slots):
                channel = allocation_ref[slot, 2 * pair + owner]
                wanted = jnp.where(channel >= 0, 2 * channel, -2 * count * rows)
                chosen.append(jnp.where(offset == wanted, 1.0, 0.0))
        hot[pl.ds(pl.multiple_of(pair * group, group), group)] = jnp.concatenate(
            chosen, axis=0
        ).astype(jnp.bfloat16)

    frame_loop(
        (high_hbm, low_hbm), volts_hbm, (high, low), frames, table_sems, frame_sems,
        total, 0, choose,
    )
    for t in range(count):
        spectra[pl.ds(t * rows, rows)] = total[t].astype(jnp.bfloat16)

    def write(i, _):
        at = pl.ds(pl.multiple_of(i * 4 * group, 4 * group), 4 * group)
        out_ref[at] = jnp.dot(hot[at], spectra[...], preferred_element_type=jnp.float32).astype(
            jnp.bfloat16
        )
        return 0

    lax.fori_loop(0, owners // 8, write, 0)


def filter_scratch(tables, feeds, count):
    return [pltpu.VMEM(table.shape, table.dtype) for table in tables] + [
        pltpu.VMEM((count, feeds, NFFT), jnp.bfloat16),
        pltpu.SemaphoreType.DMA((2,)),
        pltpu.SemaphoreType.DMA((count,)),
    ]


def order_kernel(order_ref, weights_ref, *out_refs):
    beams = weights_ref.shape[1]
    devices, share = order_ref.shape
    chips = len(out_refs)
    me = lax.axis_index("feed")
    chip, core = me // 2, me % 2
    numbers = order_ref[...].astype(jnp.float32).T
    of_device = lax.broadcasted_iota(jnp.int32, numbers.shape, 1)
    place = lax.broadcasted_iota(jnp.int32, (share, beams), 1)
    for ahead, out_ref in enumerate(out_refs):
        to = lax.rem(chip + ahead, chips)
        hot = []
        for other in range(2):
            device = 2 * to + (core if other == 0 else 1 - core)
            wanted = jnp.sum(jnp.where(of_device == device, numbers, 0.0), axis=1, keepdims=True)
            hot.append(jnp.where(place == wanted.astype(jnp.int32), 1.0, 0.0).astype(jnp.bfloat16))
        hot = jnp.concatenate(hot, axis=0)
        for part in range(2):
            rows = jnp.dot(hot, weights_ref[part], preferred_element_type=jnp.float32)
            rows = rows.astype(jnp.bfloat16)
            out_ref[0, part] = rows[:share]
            out_ref[1, part] = rows[share:]


def swap_parts(values, half, axis):
    count = values.shape[axis]
    place = lax.broadcasted_iota(jnp.int32, values.shape, axis)
    ahead = pltpu.roll(values, count - half, axis)
    behind = pltpu.roll(values, half, axis)
    return jnp.where(place % (2 * half) < half, ahead, -behind)


def gather_kernel(behind, half, scale, *refs):
    refs = list(refs)
    pairs = len(behind)
    block_refs = refs[: 4 * pairs]
    weight_refs = refs[4 * pairs : 6 * pairs]
    vis_hbm, power_ref, left, voltages, out, out_sems = refs[
        6 * pairs :
    ]
    slots, rows, narrow = block_refs[0].shape
    width = 2 * narrow
    chips = vis_hbm.shape[3] // (2 * width)
    me = lax.axis_index("feed")
    chip, core = me // 2, me % 2

    def out_copy(pair, slot):
        to = lax.rem(chip + chips - behind[pair], chips)
        at = pl.multiple_of(to * 2 * width, 2 * width)
        return pltpu.make_async_copy(
            out.at[pair, slot],
            vis_hbm.at[slot, :, :, pl.ds(at, 2 * width)],
            out_sems.at[pair, slot],
        )

    for pair in range(pairs):
        for slot in range(slots):
            feeds = [
                jnp.concatenate(
                    [block_refs[4 * pair + 2 * i + j][slot] for j in range(2)], axis=1
                )
                for i in range(2)
            ]
            if pair == 0:
                own = feeds[0].astype(jnp.float32).T
                left[slot] = jnp.concatenate([own, swap_parts(own, half, 1)], axis=0).astype(
                    jnp.bfloat16
                )
            voltage = None if pair == 0 else voltages[slot]
            for side, at in ((0, core), (1, 1 - core)):
                product = (
                    jnp.dot(left[slot], feeds[side], preferred_element_type=jnp.float32) * scale
                )
                columns = pl.ds(pl.multiple_of(at * width, width), width)
                out[pair, slot, 0, :, columns] = product[:width]
                out[pair, slot, 1, :, columns] = product[width:]
                weight = weight_refs[2 * pair + side][0]
                weight = weight.reshape(weight.shape[0] * weight.shape[1], width)
                term = lax.dot_general(
                    feeds[side], weight, NT, preferred_element_type=jnp.float32
                )
                voltage = term if voltage is None else voltage + term
            out_copy(pair, slot).start()
            if pair < pairs - 1:
                voltages[slot] = voltage
            else:
                share = voltage.shape[1] // 2
                beam = voltage[:, :share] - swap_parts(voltage[:, share:], half, 0)
                power_ref[pl.ds(slot, 1), :] = jnp.sum(beam * beam, axis=0, keepdims=True) * scale
    for pair in range(pairs):
        for slot in range(slots):
            out_copy(pair, slot).wait()


def params():
    return pltpu.CompilerParams(vmem_limit_bytes=16 * 1024 * 1024)


def gather_call(behind, half, scale, devices, blocks, weights):
    pairs = len(behind)
    slots, rows, narrow = blocks[0].shape
    width = 2 * narrow
    _, parts, share, _ = weights[0].shape
    anywhere = pl.BlockSpec(memory_space=pl.ANY)
    args = list(blocks) + list(weights)
    flops = pairs * 4 * slots * rows * width * (2 * width + parts * share)
    moved = pairs * slots * 2 * width * 2 * width * 4 + 6 * slots * rows * width
    return pl.pallas_call(
        functools.partial(gather_kernel, behind, half, scale),
        out_shape=[
            jax.ShapeDtypeStruct((slots, 2, width, devices * width), jnp.float32),
            jax.ShapeDtypeStruct((slots, share), jnp.float32),
        ],
        in_specs=[pl.BlockSpec(memory_space=pltpu.VMEM)] * len(args),
        out_specs=[anywhere, pl.BlockSpec(memory_space=pltpu.VMEM)],
        scratch_shapes=[
            pltpu.VMEM((slots, 2 * width, rows), jnp.bfloat16),
            pltpu.VMEM((slots, rows, parts * share), jnp.float32),
            pltpu.VMEM((pairs, slots, 2, width, 2 * width), jnp.float32),
            pltpu.SemaphoreType.DMA((pairs, slots)),
        ],
        compiler_params=pltpu.CompilerParams(vmem_limit_bytes=36 * 1024 * 1024),
        cost_estimate=pl.CostEstimate(flops=flops, bytes_accessed=moved, transcendentals=0),
        name="gathered",
    )(*args)


def shards(volts, beam_weights, allocation, beam_order):
    feeds_dev = volts.shape[0]
    frames_dev = volts.shape[1] // NFFT
    owners = lax.axis_size("freq")
    devices = lax.axis_size("feed")
    total_frames = frames_dev * owners
    slots_dev = allocation.shape[1]
    channels = (slots_dev - 1) * allocation.shape[0]
    rows = 2 * channels
    late = TAPS - 1
    early = frames_dev - late
    beams = beam_weights.shape[1]
    share = beams // devices
    f32, bf16 = jnp.float32, jnp.bfloat16
    tables = [jnp.asarray(x) for x in tap_transform(channels)]
    frame_flops = 4 * tables[0].shape[0] * feeds_dev * NFFT
    anywhere = pl.BlockSpec(memory_space=pl.ANY)
    in_vmem = pl.BlockSpec(memory_space=pltpu.VMEM)

    def moved(x, by):
        return lax.ppermute(x, "feed", [(i, (i + by) % devices) for i in range(devices)])

    def swapped(x):
        return lax.ppermute(x, "feed", [(i, i ^ 1) for i in range(devices)])

    own_last, next_first = pl.pallas_call(
        functools.partial(last_frames_kernel, early),
        out_shape=[jax.ShapeDtypeStruct((late, rows, feeds_dev), f32)] * 2,
        in_specs=[anywhere] * 3,
        out_specs=[in_vmem, in_vmem],
        scratch_shapes=[pltpu.VMEM((2 * late, rows, feeds_dev), f32)]
        + filter_scratch(tables, feeds_dev, late),
        compiler_params=pltpu.CompilerParams(vmem_limit_bytes=WIDE_VMEM),
        cost_estimate=pl.CostEstimate(
            flops=late * frame_flops, bytes_accessed=late * feeds_dev * NFFT * 2, transcendentals=0
        ),
        name="last_frames",
    )(*tables, volts)
    carry = lax.ppermute(next_first, "freq", [(i, i + 1) for i in range(owners - 1)])
    ordered = pl.pallas_call(
        order_kernel,
        out_shape=[jax.ShapeDtypeStruct((2, 2, share, feeds_dev), bf16)] * (devices // 2),
        compiler_params=params(),
        cost_estimate=pl.CostEstimate(
            flops=4 * beams * beams * feeds_dev, bytes_accessed=4 * beams * feeds_dev, transcendentals=0
        ),
        name="order_beams",
    )(beam_order.reshape(devices, share), beam_weights)
    own_last, *ordered = lax.optimization_barrier((own_last, *ordered))
    weights = [ordered[0], moved(ordered[1], 2), moved(ordered[3], -2), moved(ordered[2], 4)]
    chosen_rows = owners * slots_dev * 2 * frames_dev
    outgoing = pl.pallas_call(
        first_frames_kernel,
        out_shape=jax.ShapeDtypeStruct((chosen_rows, feeds_dev), bf16),
        in_specs=[anywhere] * 4 + [in_vmem] * 2,
        out_specs=in_vmem,
        scratch_shapes=[
            pltpu.VMEM((frames_dev, rows, feeds_dev), f32),
            pltpu.VMEM((chosen_rows, frames_dev * rows), bf16),
            pltpu.VMEM((frames_dev * rows, feeds_dev), bf16),
            pltpu.SMEM((slots_dev, owners), jnp.int32),
            pltpu.SemaphoreType.DMA,
        ]
        + filter_scratch(tables, feeds_dev, early),
        compiler_params=pltpu.CompilerParams(vmem_limit_bytes=WIDE_VMEM),
        cost_estimate=pl.CostEstimate(
            flops=early * frame_flops, bytes_accessed=early * feeds_dev * NFFT * 2, transcendentals=0
        ),
        name="first_frames",
    )(allocation.T, *tables, volts, own_last, carry)
    outgoing, weights[3] = lax.optimization_barrier((outgoing, weights[3]))
    received = lax.all_to_all(
        outgoing.reshape(owners, slots_dev, 2 * frames_dev, feeds_dev),
        "freq",
        split_axis=0,
        concat_axis=0,
        tiled=True,
    )

    weights_other = [swapped(weights[0][1:]), None, None, swapped(weights[3][1:])]
    received, weights[1], weights[2], weights_other[0], weights_other[3] = lax.optimization_barrier(
        (received, weights[1], weights[2], weights_other[0], weights_other[3])
    )

    own = received.transpose(1, 0, 2, 3).reshape(slots_dev, 2 * total_frames, feeds_dev)
    narrow = feeds_dev // 2
    own = [own[:, :, :narrow], own[:, :, narrow:]]
    up = [moved(own[0], 2)]
    down = [None, moved(own[1], -2)]
    up.append(moved(own[1], 2))
    down[0] = moved(own[0], -2)
    far = [moved(up[0], 2), moved(down[1], -2)]
    up[1], down[0], weights[1], weights[2] = lax.optimization_barrier(
        (up[1], down[0], weights[1], weights[2])
    )
    sibling = [swapped(x) for x in own]
    up_other = [swapped(x) for x in up]
    down_other = [swapped(x) for x in down]
    weights_other[1:3] = [swapped(x[1:]) for x in weights[1:3]]
    far_other = [swapped(x) for x in far]
    by_chip = [[weights[d], weights_other[d]] for d in range(4)]
    vis, power = gather_call(
        (0, 1, -1, 2),
        half=frames_dev,
        scale=1.0 / total_frames,
        devices=devices,
        blocks=own + sibling + up + up_other + down + down_other + far + far_other,
        weights=[x for d in range(4) for x in by_chip[d]],
    )
    return (vis, power.T)


def solution(mesh):
    in_specs = (P("feed", "freq"), P(None, None, "feed"), P(), P())
    out_specs = (P("freq", None, "feed", None), P("feed", "freq"))
    return jax.shard_map(shards, mesh=mesh, in_specs=in_specs, out_specs=out_specs, check_vma=False)
```

```python
import functools
import math

import jax
import jax.numpy as jnp
import ml_dtypes
import numpy as np
from jax import lax
from jax.experimental import pallas as pl
from jax.experimental.pallas import tpu as pltpu
from jax.sharding import PartitionSpec as P

NFFT = 2048
TAPS = 4
AHEAD = 2
FILTER_VMEM = 50 * 1024 * 1024
NT = (((1,), (1,)), ((), ()))


def tap_transform(channels):
    length = TAPS * NFFT
    positions = np.arange(length, dtype=np.float64)
    coeffs = np.sinc((positions - 0.5 * length + 0.5) / NFFT)
    coeffs = coeffs * (0.5 - 0.5 * np.cos(2.0 * math.pi * (positions + 0.5) / length))
    coeffs = coeffs * np.sqrt(NFFT / np.sum(coeffs * coeffs))
    coeffs = coeffs.reshape(TAPS, NFFT)
    angles = (np.arange(channels)[:, None] * np.arange(NFFT)[None, :] % NFFT) * (2.0 * math.pi / NFFT)
    rows = np.stack([np.cos(angles), -np.sin(angles)], axis=1) / math.sqrt(NFFT)
    rows = rows.reshape(2 * channels, NFFT)
    full = (coeffs[:, None, :] * rows[None]).reshape(TAPS * 2 * channels, NFFT)
    high = full.astype(ml_dtypes.bfloat16)
    low = (full - high.astype(np.float64)).astype(ml_dtypes.bfloat16)
    return np.concatenate([high, low], axis=0)


def frame_loop(table, volts_hbm, frames, frame_sems, total_ref, first, extra):
    half = table.shape[0] // 2
    count = frames.shape[0]
    rows = total_ref.shape[1]

    def frame_copy(i):
        at = pl.multiple_of((first + i) * NFFT, NFFT)
        return pltpu.make_async_copy(
            volts_hbm.at[:, pl.ds(at, NFFT)], frames.at[i], frame_sems.at[i]
        )

    for i in range(AHEAD):
        frame_copy(i).start()
    def step(i, _):
        @pl.when(i + AHEAD < count)
        def _():
            frame_copy(i + AHEAD).start()

        frame_copy(i).wait()
        frame = frames[i]
        product = lax.dot_general(table[:half], frame, NT, preferred_element_type=jnp.float32)
        product = product + lax.dot_general(
            table[half:], frame, NT, preferred_element_type=jnp.float32
        )
        for tap in range(TAPS):
            at = i + TAPS - 1 - tap
            total_ref[at] = total_ref[at] + product[tap * rows : (tap + 1) * rows]
        extra(i)
        return 0

    lax.fori_loop(0, count, step, 0)


def last_frames_kernel(
    first, table, volts_hbm, own_ref, next_ref, total, frames, frame_sems
):
    total[...] = jnp.zeros_like(total)
    frame_loop(
        table, volts_hbm, frames, frame_sems, total, first, lambda i: None
    )
    own_ref[...] = total[: TAPS - 1]
    next_ref[...] = total[TAPS - 1 :]


def first_frames_kernel(
    allocation_hbm, table, volts_hbm, last_ref, carry_ref, out_ref,
    total, hot, spectra, allocation_ref, allocation_sem, frames, frame_sems,
):
    allocation_copy = pltpu.make_async_copy(allocation_hbm, allocation_ref, allocation_sem)
    allocation_copy.start()
    count, rows, width = total.shape
    slots, owners = allocation_ref.shape
    late = last_ref.shape[0]
    done = count - late
    total[:late] = carry_ref[...]
    total[late:done] = jnp.zeros((done - late, rows, width), jnp.float32)
    total[done:] = last_ref[...]
    size = 2 * count
    group = 2 * slots * size
    shape = (size, count * rows)
    row = lax.broadcasted_iota(jnp.int32, shape, 0)
    part = (row >= count).astype(jnp.int32)
    offset = lax.broadcasted_iota(jnp.int32, shape, 1) - (row - part * count) * rows - part

    allocation_copy.wait()

    def choose(i):
        pair = jnp.minimum(i, owners // 2 - 1)
        chosen = []
        for owner in range(2):
            for slot in range(slots):
                channel = allocation_ref[slot, 2 * pair + owner]
                wanted = jnp.where(channel >= 0, 2 * channel, -2 * count * rows)
                chosen.append(jnp.where(offset == wanted, 1.0, 0.0))
        hot[pl.ds(pl.multiple_of(pair * group, group), group)] = jnp.concatenate(
            chosen, axis=0
        ).astype(jnp.bfloat16)

    frame_loop(
        table, volts_hbm, frames, frame_sems, total, 0, choose
    )
    for t in range(count):
        spectra[pl.ds(t * rows, rows)] = total[t].astype(jnp.bfloat16)

    def write(i, _):
        at = pl.ds(pl.multiple_of(i * 4 * group, 4 * group), 4 * group)
        out_ref[at] = jnp.dot(hot[at], spectra[...], preferred_element_type=jnp.float32).astype(
            jnp.bfloat16
        )
        return 0

    lax.fori_loop(0, owners // 8, write, 0)


def filter_scratch(feeds, count):
    return [
        pltpu.VMEM((count, feeds, NFFT), jnp.bfloat16),
        pltpu.SemaphoreType.DMA((count,)),
    ]


def order_kernel(order_ref, weights_ref, *out_refs):
    beams = weights_ref.shape[1]
    devices, share = order_ref.shape
    chips = len(out_refs)
    me = lax.axis_index("feed")
    chip, core = me // 2, me % 2
    numbers = order_ref[...].astype(jnp.float32).T
    of_device = lax.broadcasted_iota(jnp.int32, numbers.shape, 1)
    place = lax.broadcasted_iota(jnp.int32, (share, beams), 1)
    for ahead, out_ref in enumerate(out_refs):
        to = lax.rem(chip + ahead, chips)
        hot = []
        for other in range(2):
            device = 2 * to + (core if other == 0 else 1 - core)
            wanted = jnp.sum(jnp.where(of_device == device, numbers, 0.0), axis=1, keepdims=True)
            hot.append(jnp.where(place == wanted.astype(jnp.int32), 1.0, 0.0).astype(jnp.bfloat16))
        hot = jnp.concatenate(hot, axis=0)
        for part in range(2):
            rows = jnp.dot(hot, weights_ref[part], preferred_element_type=jnp.float32)
            rows = rows.astype(jnp.bfloat16)
            out_ref[0, part] = rows[:share]
            out_ref[1, part] = rows[share:]


def swap_parts(values, half, axis):
    count = values.shape[axis]
    place = lax.broadcasted_iota(jnp.int32, values.shape, axis)
    ahead = pltpu.roll(values, count - half, axis)
    behind = pltpu.roll(values, half, axis)
    return jnp.where(place % (2 * half) < half, ahead, -behind)


def gather_kernel(behind, half, scale, *refs):
    refs = list(refs)
    pairs = len(behind)
    block_refs = refs[: 4 * pairs]
    weight_refs = refs[4 * pairs : 6 * pairs]
    vis_hbm, power_ref, left, voltages, out, out_sems = refs[
        6 * pairs :
    ]
    slots, rows, narrow = block_refs[0].shape
    width = 2 * narrow
    chips = vis_hbm.shape[3] // (2 * width)
    me = lax.axis_index("feed")
    chip, core = me // 2, me % 2

    def out_copy(pair, slot):
        to = lax.rem(chip + chips - behind[pair], chips)
        at = pl.multiple_of(to * 2 * width, 2 * width)
        return pltpu.make_async_copy(
            out.at[pair, slot],
            vis_hbm.at[slot, :, :, pl.ds(at, 2 * width)],
            out_sems.at[pair, slot],
        )

    for pair in range(pairs):
        for slot in range(slots):
            feeds = [
                jnp.concatenate(
                    [block_refs[4 * pair + 2 * i + j][slot] for j in range(2)], axis=1
                )
                for i in range(2)
            ]
            if pair == 0:
                own = feeds[0].astype(jnp.float32).T
                left[slot] = jnp.concatenate([own, swap_parts(own, half, 1)], axis=0).astype(
                    jnp.bfloat16
                )
            voltage = None if pair == 0 else voltages[slot]
            for side, at in ((0, core), (1, 1 - core)):
                product = (
                    jnp.dot(left[slot], feeds[side], preferred_element_type=jnp.float32) * scale
                )
                columns = pl.ds(pl.multiple_of(at * width, width), width)
                out[pair, slot, 0, :, columns] = product[:width]
                out[pair, slot, 1, :, columns] = product[width:]
                weight = weight_refs[2 * pair + side][0]
                weight = weight.reshape(weight.shape[0] * weight.shape[1], width)
                term = lax.dot_general(
                    feeds[side], weight, NT, preferred_element_type=jnp.float32
                )
                voltage = term if voltage is None else voltage + term
            out_copy(pair, slot).start()
            if pair < pairs - 1:
                voltages[slot] = voltage
            else:
                share = voltage.shape[1] // 2
                beam = voltage[:, :share] - swap_parts(voltage[:, share:], half, 0)
                power_ref[pl.ds(slot, 1), :] = jnp.sum(beam * beam, axis=0, keepdims=True) * scale
    for pair in range(pairs):
        for slot in range(slots):
            out_copy(pair, slot).wait()


def params():
    return pltpu.CompilerParams(vmem_limit_bytes=16 * 1024 * 1024)


def gather_call(behind, half, scale, devices, blocks, weights):
    pairs = len(behind)
    slots, rows, narrow = blocks[0].shape
    width = 2 * narrow
    _, parts, share, _ = weights[0].shape
    anywhere = pl.BlockSpec(memory_space=pl.ANY)
    args = list(blocks) + list(weights)
    flops = pairs * 4 * slots * rows * width * (2 * width + parts * share)
    moved = pairs * slots * 2 * width * 2 * width * 4 + 6 * slots * rows * width
    return pl.pallas_call(
        functools.partial(gather_kernel, behind, half, scale),
        out_shape=[
            jax.ShapeDtypeStruct((slots, 2, width, devices * width), jnp.float32),
            jax.ShapeDtypeStruct((slots, share), jnp.float32),
        ],
        in_specs=[pl.BlockSpec(memory_space=pltpu.VMEM)] * len(args),
        out_specs=[anywhere, pl.BlockSpec(memory_space=pltpu.VMEM)],
        scratch_shapes=[
            pltpu.VMEM((slots, 2 * width, rows), jnp.bfloat16),
            pltpu.VMEM((slots, rows, parts * share), jnp.float32),
            pltpu.VMEM((pairs, slots, 2, width, 2 * width), jnp.float32),
            pltpu.SemaphoreType.DMA((pairs, slots)),
        ],
        compiler_params=pltpu.CompilerParams(vmem_limit_bytes=36 * 1024 * 1024),
        cost_estimate=pl.CostEstimate(flops=flops, bytes_accessed=moved, transcendentals=0),
        name="gathered",
    )(*args)


def shards(volts, beam_weights, allocation, beam_order):
    feeds_dev = volts.shape[0]
    frames_dev = volts.shape[1] // NFFT
    owners = lax.axis_size("freq")
    devices = lax.axis_size("feed")
    total_frames = frames_dev * owners
    slots_dev = allocation.shape[1]
    channels = (slots_dev - 1) * allocation.shape[0]
    rows = 2 * channels
    late = TAPS - 1
    early = frames_dev - late
    beams = beam_weights.shape[1]
    share = beams // devices
    f32, bf16 = jnp.float32, jnp.bfloat16
    table = jnp.asarray(tap_transform(channels))
    frame_flops = 2 * table.shape[0] * feeds_dev * NFFT
    anywhere = pl.BlockSpec(memory_space=pl.ANY)
    in_vmem = pl.BlockSpec(memory_space=pltpu.VMEM)

    def moved(x, by):
        return lax.ppermute(x, "feed", [(i, (i + by) % devices) for i in range(devices)])

    def swapped(x):
        return lax.ppermute(x, "feed", [(i, i ^ 1) for i in range(devices)])

    own_last, next_first = pl.pallas_call(
        functools.partial(last_frames_kernel, early),
        out_shape=[jax.ShapeDtypeStruct((late, rows, feeds_dev), f32)] * 2,
        in_specs=[in_vmem, anywhere],
        out_specs=[in_vmem, in_vmem],
        scratch_shapes=[pltpu.VMEM((2 * late, rows, feeds_dev), f32)]
        + filter_scratch(feeds_dev, late),
        compiler_params=pltpu.CompilerParams(vmem_limit_bytes=FILTER_VMEM),
        cost_estimate=pl.CostEstimate(
            flops=late * frame_flops, bytes_accessed=late * feeds_dev * NFFT * 2, transcendentals=0
        ),
        name="last_frames",
    )(table, volts)
    carry = lax.ppermute(next_first, "freq", [(i, i + 1) for i in range(owners - 1)])
    ordered = pl.pallas_call(
        order_kernel,
        out_shape=[jax.ShapeDtypeStruct((2, 2, share, feeds_dev), bf16)] * (devices // 2),
        compiler_params=params(),
        cost_estimate=pl.CostEstimate(
            flops=4 * beams * beams * feeds_dev, bytes_accessed=4 * beams * feeds_dev, transcendentals=0
        ),
        name="order_beams",
    )(beam_order.reshape(devices, share), beam_weights)
    own_last, *ordered = lax.optimization_barrier((own_last, *ordered))
    weights = [ordered[0], moved(ordered[1], 2), moved(ordered[3], -2), moved(ordered[2], 4)]
    chosen_rows = owners * slots_dev * 2 * frames_dev
    outgoing = pl.pallas_call(
        first_frames_kernel,
        out_shape=jax.ShapeDtypeStruct((chosen_rows, feeds_dev), bf16),
        in_specs=[anywhere, in_vmem, anywhere, in_vmem, in_vmem],
        out_specs=in_vmem,
        scratch_shapes=[
            pltpu.VMEM((frames_dev, rows, feeds_dev), f32),
            pltpu.VMEM((chosen_rows, frames_dev * rows), bf16),
            pltpu.VMEM((frames_dev * rows, feeds_dev), bf16),
            pltpu.SMEM((slots_dev, owners), jnp.int32),
            pltpu.SemaphoreType.DMA,
        ]
        + filter_scratch(feeds_dev, early),
        compiler_params=pltpu.CompilerParams(vmem_limit_bytes=FILTER_VMEM),
        cost_estimate=pl.CostEstimate(
            flops=early * frame_flops, bytes_accessed=early * feeds_dev * NFFT * 2, transcendentals=0
        ),
        name="first_frames",
    )(allocation.T, table, volts, own_last, carry)
    outgoing, weights[3] = lax.optimization_barrier((outgoing, weights[3]))
    received = lax.all_to_all(
        outgoing.reshape(owners, slots_dev, 2 * frames_dev, feeds_dev),
        "freq",
        split_axis=0,
        concat_axis=0,
        tiled=True,
    )

    weights_other = [swapped(weights[0][1:]), None, None, swapped(weights[3][1:])]
    received, weights[1], weights[2], weights_other[0], weights_other[3] = lax.optimization_barrier(
        (received, weights[1], weights[2], weights_other[0], weights_other[3])
    )

    own = received.transpose(1, 0, 2, 3).reshape(slots_dev, 2 * total_frames, feeds_dev)
    narrow = feeds_dev // 2
    own = [own[:, :, :narrow], own[:, :, narrow:]]
    up = [moved(own[0], 2)]
    down = [None, moved(own[1], -2)]
    up.append(moved(own[1], 2))
    down[0] = moved(own[0], -2)
    far = [moved(up[0], 2), moved(down[1], -2)]
    up[1], down[0], weights[1], weights[2] = lax.optimization_barrier(
        (up[1], down[0], weights[1], weights[2])
    )
    sibling = [swapped(x) for x in own]
    up_other = [swapped(x) for x in up]
    down_other = [swapped(x) for x in down]
    weights_other[1:3] = [swapped(x[1:]) for x in weights[1:3]]
    far_other = [swapped(x) for x in far]
    by_chip = [[weights[d], weights_other[d]] for d in range(4)]
    vis, power = gather_call(
        (0, 1, -1, 2),
        half=frames_dev,
        scale=1.0 / total_frames,
        devices=devices,
        blocks=own + sibling + up + up_other + down + down_other + far + far_other,
        weights=[x for d in range(4) for x in by_chip[d]],
    )
    return (vis, power.T)


def solution(mesh):
    in_specs = (P("feed", "freq"), P(None, None, "feed"), P(), P())
    out_specs = (P("freq", None, "feed", None), P("feed", "freq"))
    return jax.shard_map(shards, mesh=mesh, in_specs=in_specs, out_specs=out_specs, check_vma=False)
```
